32 devices in a mesh: row: 4 (over z), col: 8 (over y, x, core).
Axes of the slice: x: 2, y: 2, z: 4, core: 2. Of those that a mesh axis runs over, the one named last changes fastest.
Arguments:
- gradient: bfloat16 [8192, 8192], P('row', 'col'), may hold values from -1.5 to 1.5
- stat_old: float32 [8192, 8192], P('row', 'col'), may hold values from -6 to 6
- inv_root: bfloat16 [8192, 8192], P('row'), may hold values from -0.0625 to 0.0625
Outputs:
- stat_new: float32 [8192, 8192], P('row', 'col')
- preconditioned: bfloat16 [8192, 8192], P('row', 'col')
The draws below stay inside these ranges and needn't reach their ends.
All inputs are finite; a program needn't handle non-finite values.
Results may differ from the reference program's by a relative error of at most 0.012.
Values may be sent and summed in bfloat16 or wider, within the bound.
A program may use at most 192 MiB of HBM per device.

```python
import jax
import jax.numpy as jnp
from jax import lax

D = 8192
LAT = 8192


def levels(own_key, dims, pieces, least, largest):
    factor_of, own = 1.0, jax.random.fold_in(own_key, 6)
    for dim, blocks in pieces:
        draws = jnp.exp(jax.random.uniform(jax.random.fold_in(own, dim), (blocks,), jnp.float32, least / len(pieces), largest / len(pieces)))
        factor_of = factor_of * jnp.repeat(draws, dims[dim] // blocks).reshape([-1 if axis == dim else 1 for axis in range(len(dims))])
    return factor_of


def gaussian(rng, dims, scale, bound, cuts=(), held_as=jnp.bfloat16):
    entries = jax.random.normal(rng, dims, jnp.float32) * scale
    if len(cuts) > 0:
        entries = levels(rng, dims, cuts, -0.22, 0.18) * entries
    return jnp.clip(entries, min=-bound, max=bound).astype(held_as)


def setup_inputs(seed: int = 0) -> dict:
    arg_keys = jax.random.split(jax.random.key(seed), 4)
    return {
        "gradient": gaussian(arg_keys[0], (D, LAT), 0.25, 1.5, ((0, 4), (1, 8))),
        "stat_old": gaussian(arg_keys[1], (D, D), 1.0, 6.0, ((0, 4), (1, 8)), jnp.float32),
        "inv_root": gaussian(arg_keys[2], (D, D), D ** -0.5, 0.0625, ((0, 4),)),
    }


def reference(gradient, stat_old, inv_root):
    wide = gradient.astype(jnp.float32)
    gram = jnp.dot(wide, wide.T, precision=lax.Precision.HIGHEST, preferred_element_type=jnp.float32)
    stat_new = 0.9 * stat_old + 0.1 * gram
    product = jnp.dot(inv_root.astype(jnp.float32), wide, precision=lax.Precision.HIGHEST, preferred_element_type=jnp.float32)
    return stat_new, product.astype(jnp.bfloat16)
```

```python
import functools

import jax
import jax.numpy as jnp
from jax import lax
from jax.experimental import pallas as pl
from jax.experimental.pallas import tpu as pltpu
from jax.sharding import PartitionSpec as P

MESH = pl.DeviceIdType.MESH
WIDE = 128
NT = (((1,), (1,)), ((), ()))


def plan(nr):
    units = [(nr - 1, 2), (0, 0)]
    for place in range(1, nr - 1):
        for step in range(2, nr):
            if 2 * (step - 1) % (nr - 1) == place:
                units.append((step - 1, 2 * (step - 1) // (nr - 1)))
    return units


def kernel(nr, nc, m, tile, g_ref, r_ref, share_ref, out_ref, gv, acc, cols, rbuf, part, got, pair, heap, stage,
           zs, zr, rs, ps, pr, ss, sr, ts, ls):
    rows = gv.shape[0]
    sub = rows // 2
    chunks = sub // m
    nq = nc // 2
    z, c = lax.axis_index("row"), lax.axis_index("col")
    q, k = c // 2, c % 2
    right, left = lax.rem(z + 1, nr), lax.rem(z + nr - 1, nr)
    mate = 2 * q + (1 - k)

    barrier = pltpu.get_barrier_semaphore()
    others = [(right, c), (left, c), (z, mate)]
    others += [(z, 2 * lax.rem(q + i, nq) + k) for i in range(1, nq)]
    for other in others:
        pl.semaphore_signal(barrier, inc=1, device_id=other, device_id_type=MESH)
    pl.semaphore_wait(barrier, len(others))

    def at(j):
        return pl.ds(pl.multiple_of(j * m, m), m)

    def ring(j, step):
        src = g_ref.at[:, at(j)] if step == 1 else cols.at[j, step - 2]
        return pltpu.make_async_remote_copy(
            src_ref=src, dst_ref=cols.at[j, step - 1], send_sem=zs.at[j, step - 1], recv_sem=zr.at[j, step - 1],
            device_id=(right, c), device_id_type=MESH)

    def weights(i, step, j, h):
        block = lax.rem(z + nr - step, nr)
        first = pl.multiple_of((2 * block + h) * sub + j * m, m)
        return pltpu.make_async_copy(
            r_ref.at[:, pl.ds(first, m)], rbuf.at[i, :, pl.ds(h * m, m)], rs.at[i, h])

    def swap(i):
        return pltpu.make_async_remote_copy(
            src_ref=part.at[i, 1 - k], dst_ref=got.at[i], send_sem=ps.at[i], recv_sem=pr.at[i],
            device_id=(z, mate), device_id_type=MESH)

    def spread(i, step, j):
        block = lax.rem(z + nr - step, nr)
        return pltpu.make_async_remote_copy(
            src_ref=pair.at[i], dst_ref=heap.at[j, q], send_sem=ss.at[i], recv_sem=sr.at[j, q],
            device_id=(z, 2 * block + k), device_id_type=MESH)

    def store(j):
        return pltpu.make_async_copy(stage.at[j % 2], share_ref.at[:, at(j)], ts.at[j % 2])

    units = plan(nr)
    ring(0, 1).start()
    if chunks > 1:
        ring(1, 1).start()
    whole = [pltpu.make_async_copy(g_ref.at[h], gv.at[pl.ds(h * sub, sub)], ls.at[h]) for h in range(2)]
    for copy in whole:
        copy.start()
    for i, (step, _) in enumerate(units):
        for h in range(2):
            weights(i, step, 0, h).start()

    def clear(t, _):
        acc[pl.ds(pl.multiple_of(t * tile, tile), tile)] = jnp.zeros((tile, acc.shape[1]), jnp.float32)
        return 0

    lax.fori_loop(0, rows // tile, clear, 0)
    for copy in whole:
        copy.wait()

    def work(i, step, j):
        block = lax.rem(z + nr - step, nr)
        if step > 0:
            ring(j, step).wait_recv()
            if step < nr - 1:
                ring(j, step + 1).start()

        def read():
            if step > 0:
                return cols[j, step - 1].reshape(2 * m, gv.shape[1])
            return jnp.concatenate([gv[pl.ds(pl.multiple_of(h * sub + j * m, m), m)] for h in range(2)], axis=0)

        def gram(t, _):
            here = pl.ds(pl.multiple_of(t * tile, tile), tile)
            both = lax.dot_general(gv[here], read(), NT, preferred_element_type=jnp.float32).astype(jnp.bfloat16)
            part[i, 0, here] = both[:, :m]
            part[i, 1, here] = both[:, m:]
            return 0

        lax.fori_loop(0, rows // tile, gram, 0)
        swap(i).start()
        for h in range(2):
            weights(i, step, j, h).wait()

        def precondition(t, _):
            here = pl.ds(pl.multiple_of(t * tile, tile), tile)
            acc[here] += jnp.dot(rbuf[i, here], read(), preferred_element_type=jnp.float32)
            return 0

        lax.fori_loop(0, rows // tile, precondition, 0)

        @pl.when(j + 1 < chunks)
        def _():
            for h in range(2):
                weights(i, step, j + 1, h).start()

        swap(i).wait()

        def add(t, _):
            here = pl.ds(pl.multiple_of(t * tile, tile), tile)
            value = part[i, k, here].astype(jnp.float32) + got[i, here].astype(jnp.float32)
            return here, value.astype(jnp.bfloat16)

        @pl.when(block == q)
        def _():
            def keep(t, _):
                here, value = add(t, 0)
                heap[j, q, here] = value
                return 0

            lax.fori_loop(0, rows // tile, keep, 0)

        @pl.when(block != q)
        def _():
            @pl.when(j > 0)
            def _():
                spread(i, step, j - 1).wait_send()

            def give(t, _):
                here, value = add(t, 0)
                pair[i, here] = value
                return 0

            lax.fori_loop(0, rows // tile, give, 0)
            spread(i, step, j).start()

    def finish(j):
        for i in range(nq):
            @pl.when(i != q)
            def _():
                pltpu.make_async_remote_copy(
                    src_ref=pair.at[0], dst_ref=heap.at[j, i], send_sem=ss.at[0], recv_sem=sr.at[j, i],
                    device_id=(z, mate), device_id_type=MESH).wait_recv()

        @pl.when(j >= 2)
        def _():
            store(j - 2).wait()

        def total(t, _):
            here = pl.ds(pl.multiple_of(t * tile, tile), tile)
            value = heap[j, 0, here].astype(jnp.float32)
            for i in range(1, nq):
                value += heap[j, i, here].astype(jnp.float32)
            stage[j % 2, here] = value.astype(jnp.bfloat16)
            return 0

        lax.fori_loop(0, rows // tile, total, 0)
        store(j).start()

    def round_of(j, _):
        @pl.when((j >= 1) & (j + 1 < chunks))
        def _():
            ring(j + 1, 1).start()

        for i, (step, lag) in enumerate(units):
            @pl.when((j >= lag) & (j - lag < chunks))
            def _():
                work(i, step, j - lag)

        @pl.when(j >= 3)
        def _():
            finish(j - 3)

        return 0

    lax.fori_loop(0, chunks + 2, round_of, 0)

    def cast(t, _):
        here = pl.ds(pl.multiple_of(t * tile, tile), tile)
        gv[here] = acc[here].astype(jnp.bfloat16)
        return 0

    lax.fori_loop(0, rows // tile, cast, 0)
    result = pltpu.make_async_copy(gv, out_ref, ls.at[0])
    result.start()
    finish(chunks - 1)
    result.wait()
    if chunks > 1:
        store(chunks - 2).wait()
    store(chunks - 1).wait()
    for i, (step, _) in enumerate(units):
        @pl.when(lax.rem(z + nr - step, nr) != q)
        def _():
            spread(i, step, chunks - 1).wait_send()

    def drain(j, _):
        for step in range(1, nr):
            ring(j, step).wait_send()
        return 0

    lax.fori_loop(0, chunks, drain, 0)


def on_device(nr, nc, gradient, stat_old, inv_root):
    rows, lat = gradient.shape
    sub, m = rows // 2, WIDE
    chunks, nq = sub // m, nc // 2
    tile = min(512, rows)
    dma = pltpu.SemaphoreType.DMA
    half = jnp.bfloat16
    share, product = pl.pallas_call(
        functools.partial(kernel, nr, nc, m, tile),
        out_shape=(
            jax.ShapeDtypeStruct((rows, sub), half),
            jax.ShapeDtypeStruct((rows, lat), half),
        ),
        in_specs=[pl.BlockSpec(memory_space=pl.ANY)] * 2,
        out_specs=(pl.BlockSpec(memory_space=pl.ANY),) * 2,
        scratch_shapes=[
            pltpu.VMEM((rows, lat), half),
            pltpu.VMEM((rows, lat), jnp.float32),
            pltpu.VMEM((chunks, nr - 1, 2, m, lat), half),
            pltpu.VMEM((nr, rows, 2 * m), half),
            pltpu.VMEM((nr, 2, rows, m), half),
            pltpu.VMEM((nr, rows, m), half),
            pltpu.VMEM((nr, rows, m), half),
            pltpu.VMEM((chunks, nq, rows, m), half),
            pltpu.VMEM((2, rows, m), half),
            dma((chunks, nr - 1)),
            dma((chunks, nr - 1)),
            dma((nr, 2)),
            dma((nr,)),
            dma((nr,)),
            dma((nr,)),
            dma((chunks, nq)),
            dma((2,)),
            dma((2,)),
        ],
        compiler_params=pltpu.CompilerParams(
            collective_id=0, has_side_effects=True, vmem_limit_bytes=60 * 2**20
        ),
        cost_estimate=pl.CostEstimate(
            flops=4 * rows * lat * nr * rows, bytes_accessed=2 * rows * (2 * lat + sub + nr * rows), transcendentals=0
        ),
    )(gradient.reshape(2, sub, lat), inv_root)
    stat_new = 0.9 * stat_old + 0.1 * share.astype(jnp.float32)
    return stat_new, product


def solution(mesh):
    nr, nc = mesh.shape["row"], mesh.shape["col"]
    placed = (P("row", "col"), P("row", "col"), P("row", None))
    return jax.shard_map(
        functools.partial(on_device, nr, nc),
        mesh=mesh,
        in_specs=placed,
        out_specs=(P("row", "col"), P("row", "col")),
        check_vma=False,
    )
```

```python
import functools

import jax
import jax.numpy as jnp
from jax import lax
from jax.experimental import pallas as pl
from jax.experimental.pallas import tpu as pltpu
from jax.sharding import PartitionSpec as P

MESH = pl.DeviceIdType.MESH
WIDE = 128
NT = (((1,), (1,)), ((), ()))


def kernel(nr, nc, m, tile, g_ref, old_ref, r_ref, new_ref, out_ref, gv, acc, cols, rbuf, part, got, pair, heap, stat,
           zs, zr, rs, ps, pr, ss, sr, os, ns, ls):
    rows = gv.shape[0]
    sub = rows // 2
    chunks = sub // m
    nq = nc // 2
    z, c = lax.axis_index("row"), lax.axis_index("col")
    q, k = c // 2, c % 2
    odd = (q // 2 + q) % 2
    onward = 1 + (nr - 2) * odd
    back = nr - onward
    right, left = lax.rem(z + onward, nr), lax.rem(z + back, nr)
    mate = 2 * q + (1 - k)

    barrier = pltpu.get_barrier_semaphore()
    others = [(right, c), (left, c), (z, mate)]
    others += [(z, 2 * lax.rem(q + i, nq) + k) for i in range(1, nq)]
    for other in others:
        pl.semaphore_signal(barrier, inc=1, device_id=other, device_id_type=MESH)
    pl.semaphore_wait(barrier, len(others))

    def at(j):
        return pl.ds(pl.multiple_of(j * m, m), m)

    def ring(j, step):
        src = g_ref.at[:, at(j)] if step == 1 else cols.at[j, step - 2]
        return pltpu.make_async_remote_copy(
            src_ref=src, dst_ref=cols.at[j, step - 1], send_sem=zs.at[j, step - 1], recv_sem=zr.at[j, step - 1],
            device_id=(right, c), device_id_type=MESH)

    def weights(i, step, j, h):
        block = lax.rem(z + back * step, nr)
        first = pl.multiple_of((2 * block + h) * sub + j * m, m)
        return pltpu.make_async_copy(
            r_ref.at[:, pl.ds(first, m)], rbuf.at[i, :, pl.ds(h * m, m)], rs.at[i, h])

    def swap(i, j):
        return pltpu.make_async_remote_copy(
            src_ref=part.at[1 - k], dst_ref=got.at[j % 2, i], send_sem=ps.at[i], recv_sem=pr.at[j % 2, i],
            device_id=(z, mate), device_id_type=MESH)

    def spread(i, step, j):
        block = lax.rem(z + back * step, nr)
        return pltpu.make_async_remote_copy(
            src_ref=pair.at[i], dst_ref=heap.at[j, q], send_sem=ss.at[i], recv_sem=sr.at[j, q],
            device_id=(z, 2 * block + k), device_id_type=MESH)

    def load(j):
        return pltpu.make_async_copy(old_ref.at[:, at(j)], stat.at[j % 2], os.at[j % 2])

    def store(j):
        return pltpu.make_async_copy(stat.at[j % 2], new_ref.at[:, at(j)], ns.at[j % 2])

    ring(0, 1).start()
    whole = [pltpu.make_async_copy(g_ref.at[h], gv.at[pl.ds(h * sub, sub)], ls.at[h]) for h in range(2)]
    for copy in whole:
        copy.start()
    for step in range(nr):
        for h in range(2):
            weights(step, step, 0, h).start()
    load(0).start()

    def clear(t, _):
        acc[pl.ds(pl.multiple_of(t * tile, tile), tile)] = jnp.zeros((tile, acc.shape[1]), jnp.float32)
        return 0

    lax.fori_loop(0, rows // tile, clear, 0)
    for copy in whole:
        copy.wait()

    def work(i, step, j):
        block = lax.rem(z + back * step, nr)
        def read():
            if step > 0:
                return cols[j, step - 1].reshape(2 * m, gv.shape[1])
            return jnp.concatenate([gv[pl.ds(pl.multiple_of(h * sub + j * m, m), m)] for h in range(2)], axis=0)

        def gram(t, _):
            here = pl.ds(pl.multiple_of(t * tile, tile), tile)
            both = lax.dot_general(gv[here], read(), NT, preferred_element_type=jnp.float32).astype(jnp.bfloat16)
            part[0, here] = both[:, :m]
            part[1, here] = both[:, m:]
            return 0

        lax.fori_loop(0, rows // tile, gram, 0)
        swap(i, j).start()
        def multiply():
            for h in range(2):
                weights(i, step, j, h).wait()

            def precondition(t, _):
                here = pl.ds(pl.multiple_of(t * tile, tile), tile)
                acc[here] += jnp.dot(rbuf[i, here], read(), preferred_element_type=jnp.float32)
                return 0

            lax.fori_loop(0, rows // tile, precondition, 0)

            @pl.when(j + 1 < chunks)
            def _():
                for h in range(2):
                    weights(i, step, j + 1, h).start()

        if step < nr - 1:
            multiply()
        swap(i, j).wait()

        def add(t, _):
            here = pl.ds(pl.multiple_of(t * tile, tile), tile)
            value = part[k, here].astype(jnp.float32) + got[j % 2, i, here].astype(jnp.float32)
            return here, value.astype(jnp.bfloat16)

        @pl.when(block == q)
        def _():
            def keep(t, _):
                here, value = add(t, 0)
                heap[j, q, here] = value
                return 0

            lax.fori_loop(0, rows // tile, keep, 0)

        @pl.when(block != q)
        def _():
            @pl.when(j > 0)
            def _():
                spread(i, step, j - 1).wait_send()

            def give(t, _):
                here, value = add(t, 0)
                pair[i, here] = value
                return 0

            lax.fori_loop(0, rows // tile, give, 0)
            spread(i, step, j).start()

        if step == nr - 1:
            multiply()

    def finish(j):
        for i in range(nq):
            @pl.when(i != q)
            def _():
                pltpu.make_async_remote_copy(
                    src_ref=pair.at[0], dst_ref=heap.at[j, i], send_sem=ss.at[0], recv_sem=sr.at[j, i],
                    device_id=(z, mate), device_id_type=MESH).wait_recv()

        load(j).wait()

        def total(t, _):
            here = pl.ds(pl.multiple_of(t * tile, tile), tile)
            value = heap[j, 0, here].astype(jnp.float32)
            for i in range(1, nq):
                value += heap[j, i, here].astype(jnp.float32)
            stat[j % 2, here] = 0.9 * stat[j % 2, here] + 0.1 * value
            return 0

        lax.fori_loop(0, rows // tile, total, 0)
        store(j).start()

        @pl.when(j > 0)
        def _():
            store(j - 1).wait()

        @pl.when(j + 1 < chunks)
        def _():
            load(j + 1).start()

    def round_of(j, _):
        @pl.when(j + 1 < chunks)
        def _():
            ring(j + 1, 1).start()

        for step in range(1, nr):
            late = j - step + 1

            @pl.when((late >= 0) & (late < chunks))
            def _():
                if step < nr - 1:
                    ring(late, step).wait_recv()
                    ring(late, step + 1).start()

        for step in range(nr):
            late = j - max(step - 1, 0)

            @pl.when((late >= 0) & (late < chunks))
            def _():
                if step == nr - 1:
                    ring(late, step).wait_recv()
                work(step, step, late)

        @pl.when(j >= nr - 1)
        def _():
            finish(j - nr + 1)

        return 0

    lax.fori_loop(0, chunks + nr - 2, round_of, 0)

    def cast(t, _):
        here = pl.ds(pl.multiple_of(t * tile, tile), tile)
        gv[here] = acc[here].astype(jnp.bfloat16)
        return 0

    lax.fori_loop(0, rows // tile, cast, 0)
    result = pltpu.make_async_copy(gv, out_ref, ls.at[0])
    result.start()
    finish(chunks - 1)
    result.wait()
    store(chunks - 1).wait()
    for step in range(nr):
        @pl.when(lax.rem(z + back * step, nr) != q)
        def _():
            spread(step, step, chunks - 1).wait_send()

    def drain(j, _):
        for step in range(1, nr):
            ring(j, step).wait_send()
        return 0

    lax.fori_loop(0, chunks, drain, 0)


def on_device(nr, nc, gradient, stat_old, inv_root):
    rows, lat = gradient.shape
    sub, m = rows // 2, WIDE
    chunks, nq = sub // m, nc // 2
    tile = min(512, rows)
    dma = pltpu.SemaphoreType.DMA
    half = jnp.bfloat16
    return pl.pallas_call(
        functools.partial(kernel, nr, nc, m, tile),
        out_shape=(
            jax.ShapeDtypeStruct((rows, sub), jnp.float32),
            jax.ShapeDtypeStruct((rows, lat), half),
        ),
        in_specs=[pl.BlockSpec(memory_space=pl.ANY)] * 3,
        out_specs=(pl.BlockSpec(memory_space=pl.ANY),) * 2,
        scratch_shapes=[
            pltpu.VMEM((rows, lat), half),
            pltpu.VMEM((rows, lat), jnp.float32),
            pltpu.VMEM((chunks, nr - 1, 2, m, lat), half),
            pltpu.VMEM((nr, rows, 2 * m), half),
            pltpu.VMEM((2, rows, m), half),
            pltpu.VMEM((2, nr, rows, m), half),
            pltpu.VMEM((nr, rows, m), half),
            pltpu.VMEM((chunks, nq, rows, m), half),
            pltpu.VMEM((2, rows, m), jnp.float32),
            dma((chunks, nr - 1)),
            dma((chunks, nr - 1)),
            dma((nr, 2)),
            dma((nr,)),
            dma((2, nr)),
            dma((nr,)),
            dma((chunks, nq)),
            dma((2,)),
            dma((2,)),
            dma((2,)),
        ],
        compiler_params=pltpu.CompilerParams(
            collective_id=0, has_side_effects=True, vmem_limit_bytes=60 * 2**20
        ),
        cost_estimate=pl.CostEstimate(
            flops=4 * rows * lat * nr * rows, bytes_accessed=2 * rows * (2 * lat + 4 * sub + nr * rows), transcendentals=0
        ),
    )(gradient.reshape(2, sub, lat), stat_old, inv_root)


def solution(mesh):
    nr, nc = mesh.shape["row"], mesh.shape["col"]
    placed = (P("row", "col"), P("row", "col"), P("row", None))
    return jax.shard_map(
        functools.partial(on_device, nr, nc),
        mesh=mesh,
        in_specs=placed,
        out_specs=(P("row", "col"), P("row", "col")),
        check_vma=False,
    )
```

```python
import functools

import jax
import jax.numpy as jnp
from jax import lax
from jax.experimental import pallas as pl
from jax.experimental.pallas import tpu as pltpu
from jax.sharding import PartitionSpec as P

MESH = pl.DeviceIdType.MESH
WIDE = 128
NT = (((1,), (1,)), ((), ()))


def kernel(nr, nc, m, tile, g_ref, old_ref, r_ref, new_ref, out_ref, gv, acc, cols, rbuf, part, got, pair, relay, heap, stat,
           zs, zr, rs, ps, pr, ss, ar, sr, os, ns, ls):
    rows = gv.shape[0]
    sub = rows // 2
    chunks = sub // m
    nq = nc // 2
    z, c = lax.axis_index("row"), lax.axis_index("col")
    q, k = c // 2, c % 2
    back = nr - 1
    right, left = lax.rem(z + 1, nr), lax.rem(z + back, nr)
    mate = 2 * q + (1 - k)

    half = nq // 2

    def digit(chip):
        return (1 - k) * (chip % 2) + k * (chip // half)

    def rest(chip):
        return (1 - k) * (chip // 2) + k * (chip % half)

    across = q + (1 - 2 * digit(q)) * ((1 - k) + k * half)

    barrier = pltpu.get_barrier_semaphore()
    others = [(right, c), (left, c), (z, mate)]
    others += [(z, 2 * lax.rem(q + i, nq) + k) for i in range(1, nq)]
    for other in others:
        pl.semaphore_signal(barrier, inc=1, device_id=other, device_id_type=MESH)
    pl.semaphore_wait(barrier, len(others))

    def at(j):
        return pl.ds(pl.multiple_of(j * m, m), m)

    def ring(j, step):
        src = g_ref.at[:, at(j)] if step == 1 else cols.at[j, step - 2]
        return pltpu.make_async_remote_copy(
            src_ref=src, dst_ref=cols.at[j, step - 1], send_sem=zs.at[j, step - 1], recv_sem=zr.at[j, step - 1],
            device_id=(right, c), device_id_type=MESH)

    def weights(i, step, j, h):
        block = lax.rem(z + back * step, nr)
        first = pl.multiple_of((2 * block + h) * sub + j * m, m)
        return pltpu.make_async_copy(
            r_ref.at[:, pl.ds(first, m)], rbuf.at[i, :, pl.ds(h * m, m)], rs.at[i, h])

    def swap(i, j):
        return pltpu.make_async_remote_copy(
            src_ref=part.at[1 - k], dst_ref=got.at[j % 2, i], send_sem=ps.at[i], recv_sem=pr.at[j % 2, i],
            device_id=(z, mate), device_id_type=MESH)

    def hand(i, step, j):
        place = rest(lax.rem(z + back * step, nr))
        return pltpu.make_async_remote_copy(
            src_ref=pair.at[i], dst_ref=relay.at[j, place], send_sem=ss.at[i], recv_sem=ar.at[j, place],
            device_id=(z, 2 * across + k), device_id_type=MESH)

    def spread(i, step, j):
        block = lax.rem(z + back * step, nr)
        return pltpu.make_async_remote_copy(
            src_ref=pair.at[i], dst_ref=heap.at[j, rest(q)], send_sem=ss.at[i], recv_sem=sr.at[j, rest(q)],
            device_id=(z, 2 * block + k), device_id_type=MESH)

    def load(j):
        return pltpu.make_async_copy(old_ref.at[:, at(j)], stat.at[j % 2], os.at[j % 2])

    def store(j):
        return pltpu.make_async_copy(stat.at[j % 2], new_ref.at[:, at(j)], ns.at[j % 2])

    ring(0, 1).start()
    whole = [pltpu.make_async_copy(g_ref.at[h], gv.at[pl.ds(h * sub, sub)], ls.at[h]) for h in range(2)]
    for copy in whole:
        copy.start()
    for step in range(nr):
        for h in range(2):
            weights(step, step, 0, h).start()
    load(0).start()

    def clear(t, _):
        acc[pl.ds(pl.multiple_of(t * tile, tile), tile)] = jnp.zeros((tile, acc.shape[1]), jnp.float32)
        return 0

    lax.fori_loop(0, rows // tile, clear, 0)
    for copy in whole:
        copy.wait()

    def work(i, step, j):
        block = lax.rem(z + back * step, nr)

        def read():
            if step > 0:
                return cols[j, step - 1].reshape(2 * m, gv.shape[1])
            return jnp.concatenate([gv[pl.ds(pl.multiple_of(h * sub + j * m, m), m)] for h in range(2)], axis=0)

        def gram(t, _):
            here = pl.ds(pl.multiple_of(t * tile, tile), tile)
            both = lax.dot_general(gv[here], read(), NT, preferred_element_type=jnp.float32).astype(jnp.bfloat16)
            part[0, here] = both[:, :m]
            part[1, here] = both[:, m:]
            return 0

        lax.fori_loop(0, rows // tile, gram, 0)
        swap(i, j).start()

        def multiply():
            for h in range(2):
                weights(i, step, j, h).wait()

            def precondition(t, _):
                here = pl.ds(pl.multiple_of(t * tile, tile), tile)
                acc[here] += jnp.dot(rbuf[i, here], read(), preferred_element_type=jnp.float32)
                return 0

            lax.fori_loop(0, rows // tile, precondition, 0)

            @pl.when(j + 1 < chunks)
            def _():
                for h in range(2):
                    weights(i, step, j + 1, h).start()

        if step < nr - 1:
            multiply()
        swap(i, j).wait()

        @pl.when(j > 0)
        def _():
            sent(i, step, j - 1)

        def add(t, _):
            here = pl.ds(pl.multiple_of(t * tile, tile), tile)
            value = part[k, here].astype(jnp.float32) + got[j % 2, i, here].astype(jnp.float32)
            pair[i, here] = value.astype(jnp.bfloat16)
            return 0

        lax.fori_loop(0, rows // tile, add, 0)

        @pl.when(digit(block) != digit(q))
        def _():
            hand(i, step, j).start()

        if step == nr - 1:
            multiply()

    def sent(i, step, j):
        block = lax.rem(z + back * step, nr)

        @pl.when(digit(block) != digit(q))
        def _():
            hand(i, step, j).wait_send()

        @pl.when((digit(block) == digit(q)) & (block != q))
        def _():
            spread(i, step, j).wait_send()

    def settle(i, step, j):
        block = lax.rem(z + back * step, nr)

        def add(t):
            here = pl.ds(pl.multiple_of(t * tile, tile), tile)
            value = pair[i, here].astype(jnp.float32) + relay[j, rest(q), here].astype(jnp.float32)
            return here, value.astype(jnp.bfloat16)

        @pl.when(block == q)
        def _():
            hand(i, step, j).wait_recv()

            def keep(t, _):
                here, value = add(t)
                heap[j, rest(q), here] = value
                return 0

            lax.fori_loop(0, rows // tile, keep, 0)

        @pl.when((digit(block) == digit(q)) & (block != q))
        def _():
            hand(i, step, j).wait_recv()

            def give(t, _):
                here = pl.ds(pl.multiple_of(t * tile, tile), tile)
                value = pair[i, here].astype(jnp.float32) + relay[j, rest(block), here].astype(jnp.float32)
                pair[i, here] = value.astype(jnp.bfloat16)
                return 0

            lax.fori_loop(0, rows // tile, give, 0)
            spread(i, step, j).start()

    def finish(j):
        for i in range(half):
            @pl.when(i != rest(q))
            def _():
                pltpu.make_async_remote_copy(
                    src_ref=pair.at[0], dst_ref=heap.at[j, i], send_sem=ss.at[0], recv_sem=sr.at[j, i],
                    device_id=(z, mate), device_id_type=MESH).wait_recv()

        load(j).wait()

        def total(t, _):
            here = pl.ds(pl.multiple_of(t * tile, tile), tile)
            value = heap[j, 0, here].astype(jnp.float32)
            for i in range(1, half):
                value += heap[j, i, here].astype(jnp.float32)
            stat[j % 2, here] = 0.9 * stat[j % 2, here] + 0.1 * value
            return 0

        lax.fori_loop(0, rows // tile, total, 0)
        store(j).start()

        @pl.when(j > 0)
        def _():
            store(j - 1).wait()

        @pl.when(j + 1 < chunks)
        def _():
            load(j + 1).start()

    def round_of(j, _):
        @pl.when(j + 1 < chunks)
        def _():
            ring(j + 1, 1).start()

        for step in range(1, nr):
            late = j - step + 1

            @pl.when((late >= 0) & (late < chunks))
            def _():
                if step < nr - 1:
                    ring(late, step).wait_recv()
                    ring(late, step + 1).start()

        for step in range(nr):
            late = j - max(step - 1, 0)

            @pl.when((late >= 0) & (late < chunks))
            def _():
                if step == nr - 1:
                    ring(late, step).wait_recv()
                work(step, step, late)

            last = (step + nr - 1) % nr
            before = j - (nr - 1) if step == 0 else j - max(last - 1, 0)

            @pl.when((before >= 0) & (before < chunks))
            def _():
                settle(last, last, before)

        @pl.when(j >= nr - 1)
        def _():
            finish(j - nr + 1)

        return 0

    lax.fori_loop(0, chunks + nr - 2, round_of, 0)

    settle(nr - 1, nr - 1, chunks - 1)

    def cast(t, _):
        here = pl.ds(pl.multiple_of(t * tile, tile), tile)
        gv[here] = acc[here].astype(jnp.bfloat16)
        return 0

    lax.fori_loop(0, rows // tile, cast, 0)
    result = pltpu.make_async_copy(gv, out_ref, ls.at[0])
    result.start()
    finish(chunks - 1)
    result.wait()
    store(chunks - 1).wait()
    for step in range(nr):
        sent(step, step, chunks - 1)

    def drain(j, _):
        for step in range(1, nr):
            ring(j, step).wait_send()
        return 0

    lax.fori_loop(0, chunks, drain, 0)


def on_device(nr, nc, gradient, stat_old, inv_root):
    rows, lat = gradient.shape
    sub, m = rows // 2, WIDE
    chunks, nq = sub // m, nc // 2
    tile = min(512, rows)
    dma = pltpu.SemaphoreType.DMA
    half = jnp.bfloat16
    return pl.pallas_call(
        functools.partial(kernel, nr, nc, m, tile),
        out_shape=(
            jax.ShapeDtypeStruct((rows, sub), jnp.float32),
            jax.ShapeDtypeStruct((rows, lat), half),
        ),
        in_specs=[pl.BlockSpec(memory_space=pl.ANY)] * 3,
        out_specs=(pl.BlockSpec(memory_space=pl.ANY),) * 2,
        scratch_shapes=[
            pltpu.VMEM((rows, lat), half),
            pltpu.VMEM((rows, lat), jnp.float32),
            pltpu.VMEM((chunks, nr - 1, 2, m, lat), half),
            pltpu.VMEM((nr, rows, 2 * m), half),
            pltpu.VMEM((2, rows, m), half),
            pltpu.VMEM((2, nr, rows, m), half),
            pltpu.VMEM((nr, rows, m), half),
            pltpu.VMEM((chunks, nq // 2, rows, m), half),
            pltpu.VMEM((chunks, nq // 2, rows, m), half),
            pltpu.VMEM((2, rows, m), jnp.float32),
            dma((chunks, nr - 1)),
            dma((chunks, nr - 1)),
            dma((nr, 2)),
            dma((nr,)),
            dma((2, nr)),
            dma((nr,)),
            dma((chunks, nq // 2)),
            dma((chunks, nq // 2)),
            dma((2,)),
            dma((2,)),
            dma((2,)),
        ],
        compiler_params=pltpu.CompilerParams(
            collective_id=0, has_side_effects=True, vmem_limit_bytes=60 * 2**20
        ),
        cost_estimate=pl.CostEstimate(
            flops=4 * rows * lat * nr * rows, bytes_accessed=2 * rows * (2 * lat + 4 * sub + nr * rows), transcendentals=0
        ),
    )(gradient.reshape(2, sub, lat), stat_old, inv_root)


def solution(mesh):
    nr, nc = mesh.shape["row"], mesh.shape["col"]
    placed = (P("row", "col"), P("row", "col"), P("row", None))
    return jax.shard_map(
        functools.partial(on_device, nr, nc),
        mesh=mesh,
        in_specs=placed,
        out_specs=(P("row", "col"), P("row", "col")),
        check_vma=False,
    )
```

```python
import functools

import jax
import jax.numpy as jnp
from jax import lax
from jax.experimental import pallas as pl
from jax.experimental.pallas import tpu as pltpu
from jax.sharding import PartitionSpec as P

MESH = pl.DeviceIdType.MESH
WIDE = 128
NT = (((1,), (1,)), ((), ()))


def kernel(nr, nc, m, tile, g_ref, old_ref, r_ref, new_ref, out_ref, gv, acc, cols, rbuf, part, got, pair, relay, heap, stat,
           zs, zr, rs, ps, pr, ss, ar, sr, os, ns, ls):
    rows = gv.shape[0]
    sub = rows // 2
    steps = rows // 2 // tile
    chunks = sub // m
    nq = nc // 2
    z, c = lax.axis_index("row"), lax.axis_index("col")
    q, k = c // 2, c % 2
    back = nr - 1
    right, left = lax.rem(z + 1, nr), lax.rem(z + back, nr)
    mate = 2 * q + (1 - k)

    half = nq // 2

    def digit(chip):
        return (1 - k) * (chip % 2) + k * (chip // half)

    def rest(chip):
        return (1 - k) * (chip // 2) + k * (chip % half)

    across = q + (1 - 2 * digit(q)) * ((1 - k) + k * half)

    barrier = pltpu.get_barrier_semaphore()
    others = [(right, c), (left, c), (z, mate)]
    others += [(z, 2 * lax.rem(q + i, nq) + k) for i in range(1, nq)]
    for other in others:
        pl.semaphore_signal(barrier, inc=1, device_id=other, device_id_type=MESH)
    pl.semaphore_wait(barrier, len(others))

    def at(j):
        return pl.ds(pl.multiple_of(j * m, m), m)

    def ring(j, step):
        src = g_ref.at[:, at(j)] if step == 1 else cols.at[j, step - 2]
        return pltpu.make_async_remote_copy(
            src_ref=src, dst_ref=cols.at[j, step - 1], send_sem=zs.at[j, step - 1], recv_sem=zr.at[j, step - 1],
            device_id=(right, c), device_id_type=MESH)

    def weights(i, step, j, h):
        block = lax.rem(z + back * step, nr)
        first = pl.multiple_of((2 * block + h) * sub + j * m, m)
        return pltpu.make_async_copy(
            r_ref.at[:, pl.ds(first, m)], rbuf.at[i, :, pl.ds(h * m, m)], rs.at[i, h])

    def halves(p):
        return pl.ds(p * (rows // 2), rows // 2)

    def swap(i, j, p):
        return pltpu.make_async_remote_copy(
            src_ref=part.at[1 - k, halves(p)], dst_ref=got.at[j % 2, i, halves(p)],
            send_sem=ps.at[i, p], recv_sem=pr.at[j % 2, i, p],
            device_id=(z, mate), device_id_type=MESH)

    def hand(i, step, j, p):
        place = rest(lax.rem(z + back * step, nr))
        return pltpu.make_async_remote_copy(
            src_ref=pair.at[i, halves(p)], dst_ref=relay.at[j, place, halves(p)],
            send_sem=ss.at[i, p], recv_sem=ar.at[j, place, p],
            device_id=(z, 2 * across + k), device_id_type=MESH)

    def spread(i, step, j, p):
        block = lax.rem(z + back * step, nr)
        return pltpu.make_async_remote_copy(
            src_ref=pair.at[i, halves(p)], dst_ref=heap.at[j, rest(q), halves(p)],
            send_sem=ss.at[i, p], recv_sem=sr.at[j, rest(q), p],
            device_id=(z, 2 * block + k), device_id_type=MESH)

    def load(j):
        return pltpu.make_async_copy(old_ref.at[:, at(j)], stat.at[j % 2], os.at[j % 2])

    def store(j):
        return pltpu.make_async_copy(stat.at[j % 2], new_ref.at[:, at(j)], ns.at[j % 2])

    ring(0, 1).start()
    whole = [pltpu.make_async_copy(g_ref.at[h], gv.at[pl.ds(h * sub, sub)], ls.at[h]) for h in range(2)]
    for copy in whole:
        copy.start()
    for step in range(nr):
        for h in range(2):
            weights(step, step, 0, h).start()
    load(0).start()

    def clear(t, _):
        acc[pl.ds(pl.multiple_of(t * tile, tile), tile)] = jnp.zeros((tile, acc.shape[1]), jnp.float32)
        return 0

    lax.fori_loop(0, rows // tile, clear, 0)
    for copy in whole:
        copy.wait()

    def work(i, step, j):
        block = lax.rem(z + back * step, nr)

        def read():
            if step > 0:
                return cols[j, step - 1].reshape(2 * m, gv.shape[1])
            return jnp.concatenate([gv[pl.ds(pl.multiple_of(h * sub + j * m, m), m)] for h in range(2)], axis=0)

        def gram(t, _):
            here = pl.ds(pl.multiple_of(t * tile, tile), tile)
            both = lax.dot_general(gv[here], read(), NT, preferred_element_type=jnp.float32).astype(jnp.bfloat16)
            part[0, here] = both[:, :m]
            part[1, here] = both[:, m:]
            return 0

        for p in range(2):
            lax.fori_loop(p * steps, (p + 1) * steps, gram, 0)
            swap(i, j, p).start()

        def multiply():
            for h in range(2):
                weights(i, step, j, h).wait()

            def precondition(t, _):
                here = pl.ds(pl.multiple_of(t * tile, tile), tile)
                acc[here] += jnp.dot(rbuf[i, here], read(), preferred_element_type=jnp.float32)
                return 0

            lax.fori_loop(0, rows // tile, precondition, 0)

            @pl.when(j + 1 < chunks)
            def _():
                for h in range(2):
                    weights(i, step, j + 1, h).start()

        if step < nr - 1:
            multiply()

        @pl.when(j > 0)
        def _():
            sent(i, step, j - 1)

        def add(t, _):
            here = pl.ds(pl.multiple_of(t * tile, tile), tile)
            value = part[k, here].astype(jnp.float32) + got[j % 2, i, here].astype(jnp.float32)
            pair[i, here] = value.astype(jnp.bfloat16)
            return 0

        for p in range(2):
            swap(i, j, p).wait()
            lax.fori_loop(p * steps, (p + 1) * steps, add, 0)

            @pl.when(digit(block) != digit(q))
            def _():
                hand(i, step, j, p).start()

        if step == nr - 1:
            multiply()

    def sent(i, step, j):
        block = lax.rem(z + back * step, nr)

        @pl.when(digit(block) != digit(q))
        def _():
            for p in range(2):
                hand(i, step, j, p).wait_send()

        @pl.when((digit(block) == digit(q)) & (block != q))
        def _():
            for p in range(2):
                spread(i, step, j, p).wait_send()

    def settle(i, step, j):
        block = lax.rem(z + back * step, nr)

        def add(t):
            here = pl.ds(pl.multiple_of(t * tile, tile), tile)
            value = pair[i, here].astype(jnp.float32) + relay[j, rest(q), here].astype(jnp.float32)
            return here, value.astype(jnp.bfloat16)

        @pl.when(block == q)
        def _():
            for p in range(2):
                hand(i, step, j, p).wait_recv()

            def keep(t, _):
                here, value = add(t)
                heap[j, rest(q), here] = value
                return 0

            lax.fori_loop(0, rows // tile, keep, 0)

        @pl.when((digit(block) == digit(q)) & (block != q))
        def _():
            def give(t, _):
                here = pl.ds(pl.multiple_of(t * tile, tile), tile)
                value = pair[i, here].astype(jnp.float32) + relay[j, rest(block), here].astype(jnp.float32)
                pair[i, here] = value.astype(jnp.bfloat16)
                return 0

            for p in range(2):
                hand(i, step, j, p).wait_recv()
                lax.fori_loop(p * steps, (p + 1) * steps, give, 0)
                spread(i, step, j, p).start()

    def finish(j):
        for i in range(half):
            @pl.when(i != rest(q))
            def _():
                for p in range(2):
                    pltpu.make_async_remote_copy(
                        src_ref=pair.at[0, halves(p)], dst_ref=heap.at[j, i, halves(p)],
                        send_sem=ss.at[0, p], recv_sem=sr.at[j, i, p],
                        device_id=(z, mate), device_id_type=MESH).wait_recv()

        load(j).wait()

        def total(t, _):
            here = pl.ds(pl.multiple_of(t * tile, tile), tile)
            value = heap[j, 0, here].astype(jnp.float32)
            for i in range(1, half):
                value += heap[j, i, here].astype(jnp.float32)
            stat[j % 2, here] = 0.9 * stat[j % 2, here] + 0.1 * value
            return 0

        lax.fori_loop(0, rows // tile, total, 0)
        store(j).start()

        @pl.when(j > 0)
        def _():
            store(j - 1).wait()

        @pl.when(j + 1 < chunks)
        def _():
            load(j + 1).start()

    def round_of(j, _):
        @pl.when(j + 1 < chunks)
        def _():
            ring(j + 1, 1).start()

        for step in range(1, nr):
            late = j - step + 1

            @pl.when((late >= 0) & (late < chunks))
            def _():
                if step < nr - 1:
                    ring(late, step).wait_recv()
                    ring(late, step + 1).start()

        for step in range(nr):
            late = j - max(step - 1, 0)

            @pl.when((late >= 0) & (late < chunks))
            def _():
                if step == nr - 1:
                    ring(late, step).wait_recv()
                work(step, step, late)

            last = (step + nr - 1) % nr
            before = j - (nr - 1) if step == 0 else j - max(last - 1, 0)

            @pl.when((before >= 0) & (before < chunks))
            def _():
                settle(last, last, before)

        @pl.when(j >= nr - 1)
        def _():
            finish(j - nr + 1)

        return 0

    lax.fori_loop(0, chunks + nr - 2, round_of, 0)

    settle(nr - 1, nr - 1, chunks - 1)

    def cast(t, _):
        here = pl.ds(pl.multiple_of(t * tile, tile), tile)
        gv[here] = acc[here].astype(jnp.bfloat16)
        return 0

    lax.fori_loop(0, rows // tile, cast, 0)
    result = pltpu.make_async_copy(gv, out_ref, ls.at[0])
    result.start()
    finish(chunks - 1)
    result.wait()
    store(chunks - 1).wait()
    for step in range(nr):
        sent(step, step, chunks - 1)

    def drain(j, _):
        for step in range(1, nr):
            ring(j, step).wait_send()
        return 0

    lax.fori_loop(0, chunks, drain, 0)


def on_device(nr, nc, gradient, stat_old, inv_root):
    rows, lat = gradient.shape
    sub, m = rows // 2, WIDE
    chunks, nq = sub // m, nc // 2
    tile = min(512, rows // 2)
    dma = pltpu.SemaphoreType.DMA
    half = jnp.bfloat16
    return pl.pallas_call(
        functools.partial(kernel, nr, nc, m, tile),
        out_shape=(
            jax.ShapeDtypeStruct((rows, sub), jnp.float32),
            jax.ShapeDtypeStruct((rows, lat), half),
        ),
        in_specs=[pl.BlockSpec(memory_space=pl.ANY)] * 3,
        out_specs=(pl.BlockSpec(memory_space=pl.ANY),) * 2,
        scratch_shapes=[
            pltpu.VMEM((rows, lat), half),
            pltpu.VMEM((rows, lat), jnp.float32),
            pltpu.VMEM((chunks, nr - 1, 2, m, lat), half),
            pltpu.VMEM((nr, rows, 2 * m), half),
            pltpu.VMEM((2, rows, m), half),
            pltpu.VMEM((2, nr, rows, m), half),
            pltpu.VMEM((nr, rows, m), half),
            pltpu.VMEM((chunks, nq // 2, rows, m), half),
            pltpu.VMEM((chunks, nq // 2, rows, m), half),
            pltpu.VMEM((2, rows, m), jnp.float32),
            dma((chunks, nr - 1)),
            dma((chunks, nr - 1)),
            dma((nr, 2)),
            dma((nr, 2)),
            dma((2, nr, 2)),
            dma((nr, 2)),
            dma((chunks, nq // 2, 2)),
            dma((chunks, nq // 2, 2)),
            dma((2,)),
            dma((2,)),
            dma((2,)),
        ],
        compiler_params=pltpu.CompilerParams(
            collective_id=0, has_side_effects=True, vmem_limit_bytes=60 * 2**20
        ),
        cost_estimate=pl.CostEstimate(
            flops=4 * rows * lat * nr * rows, bytes_accessed=2 * rows * (2 * lat + 4 * sub + nr * rows), transcendentals=0
        ),
    )(gradient.reshape(2, sub, lat), stat_old, inv_root)


def solution(mesh):
    nr, nc = mesh.shape["row"], mesh.shape["col"]
    placed = (P("row", "col"), P("row", "col"), P("row", None))
    return jax.shard_map(
        functools.partial(on_device, nr, nc),
        mesh=mesh,
        in_specs=placed,
        out_specs=(P("row", "col"), P("row", "col")),
        check_vma=False,
    )
```
